128 devices in a mesh: dp: 32 (over y, x_lo, z), rep: 4 (over x_hi, core).
Axes of the slice: x: 4 (x_hi: 2, x_lo: 2; x = x_hi * 2 + x_lo), y: 4, z: 4, core: 2. Of those that a mesh axis runs over, the one named last changes fastest.
Arguments:
- images: bfloat16 [65536, 1152], P(('dp', 'rep')), may hold values from -1 to 1
- texts: bfloat16 [65536, 1152], P(('dp', 'rep')), may hold values from -1 to 1
- partner: int32 [65536], P(('dp', 'rep')), may hold values from 0 to 65535, as said below
- scale: float32 [1], replicated, may hold values from 1 to 3
- offset: float32 [1], replicated, may hold values from -2 to 0
Outputs:
- row_loss: float32 [65536], P(('dp', 'rep'))
- grad_images: bfloat16 [65536, 1152], P(('dp', 'rep'))
- grad_texts: bfloat16 [65536, 1152], P(('dp', 'rep'))
The draws below stay inside these ranges and needn't reach their ends.
Inputs may be any that keep to these rules, and one draw needn't show every extreme that they name: partner[i] lies in the block of i or in the block before it, (k - 1) mod 32; index 0 has partner 65536 - 1 and index 1 has partner 0.
All inputs are finite; a program needn't handle non-finite values.
Results may differ from the reference program's by a relative error of at most 0.0041.
Values may be sent and summed in bfloat16 or wider, within the bound.
No kernel may reach another device: no remote copies, remote signals or barrier semaphores. Data moves between devices by JAX's collectives and lax.ppermute only.
A program may use at most 128 MiB of HBM per device.

```python
import math
import jax
import jax.numpy as jnp
from jax import lax

D = 1152
TOK_DEV = 2048
TOKENS = 65536
N_DP = 32


def draw_partner(key, part):
    key = jax.random.fold_in(key, 7)
    key_side, key_row = jax.random.split(key)
    index = jnp.arange(TOKENS, dtype=jnp.int32)
    block = index // TOK_DEV
    side = jax.random.randint(key_side, (TOKENS,), 0, 2, dtype=jnp.int32)
    row = jax.random.randint(key_row, (TOKENS,), 0, TOK_DEV, dtype=jnp.int32)
    target = (block - side + N_DP) % N_DP
    result = target * TOK_DEV + row
    result = result.at[0].set(TOKENS - 1)
    result = result.at[1].set(0)
    return result.astype(jnp.int32)


def level_of(rng, extent, pieces, least, high):
    def one(position, blocks):
        steps = jax.random.uniform(jax.random.fold_in(jax.random.fold_in(rng, 6), position), (blocks,), jnp.float32, least / len(pieces), high / len(pieces))
        return jnp.repeat(jnp.exp(steps), extent[position] // blocks).reshape((-1,) + (1,) * (len(extent) - position - 1))

    level = one(*pieces[0])
    for cut in pieces[1:]:
        level = level * one(*cut)
    return level


def scatter_about(stream_key, shape, deviation, most, cuts=(), held_as=jnp.bfloat16):
    level = level_of(stream_key, shape, cuts, -0.22, 0.18) if cuts else 1.0
    values = jax.random.normal(stream_key, shape, jnp.float32) * deviation * level
    return jnp.minimum(jnp.maximum(values, -most), most).astype(held_as)


def setup_inputs(seed: int = 0) -> dict:
    key_of = jax.random.split(jax.random.key(seed), 6)
    images = scatter_about(key_of[0], (TOKENS, D), 0.17, 1.0, ((0, 128),))
    texts = scatter_about(key_of[1], (TOKENS, D), 0.17, 1.0, ((0, 128),))
    partner = draw_partner(jax.random.fold_in(key_of[5], 71), 0)
    scale = jnp.clip(jnp.exp(jax.random.uniform(key_of[3], (1,), jnp.float32, math.log(1.0), math.log(3.0))), 1.0, 3.0)
    offset = jnp.clip(jax.random.uniform(key_of[4], (1,), jnp.float32, -2.0, 0.0), -2.0, 0.0)
    return dict(images=images, texts=texts, partner=partner, scale=scale, offset=offset)


def block_terms(image_rows, text_rows, partner_rows, start, temper, shift_bias):
    logits = temper * jnp.dot(image_rows, text_rows.T, preferred_element_type=jnp.float32) + shift_bias
    columns = start + jnp.arange(text_rows.shape[0], dtype=jnp.int32)
    sign = jnp.where(partner_rows[:, None] == columns[None, :], 1.0, -1.0).astype(jnp.float32)
    loss_sum = jnp.sum(jax.nn.softplus(-sign * logits), axis=1)
    coef = (-temper * sign * jax.nn.sigmoid(-sign * logits)).astype(jnp.bfloat16)
    grad_img = jnp.dot(coef, text_rows, preferred_element_type=jnp.float32)
    grad_txt = jnp.dot(coef.T, image_rows, preferred_element_type=jnp.float32)
    return loss_sum, grad_img, grad_txt


def reference(images, texts, partner, scale, offset):
    temper = scale[0]
    shift_bias = offset[0]
    image_blocks = images.reshape(N_DP, TOK_DEV, D)
    text_blocks = texts.reshape(N_DP, TOK_DEV, D)
    prev_blocks = jnp.roll(text_blocks, 1, axis=0)
    partner_blocks = partner.reshape(N_DP, TOK_DEV)
    block_ids = jnp.arange(N_DP, dtype=jnp.int32)

    def one_block(items):
        image_rows, own_rows, prev_rows, partner_rows, index = items
        own_start = (index * TOK_DEV).astype(jnp.int32)
        prev_start = (((index + N_DP - 1) % N_DP) * TOK_DEV).astype(jnp.int32)
        loss_own, gimg_own, gtxt_own = block_terms(image_rows, own_rows, partner_rows, own_start, temper, shift_bias)
        loss_prev, gimg_prev, gtxt_prev = block_terms(image_rows, prev_rows, partner_rows, prev_start, temper, shift_bias)
        row_loss = (loss_own + loss_prev) / jnp.float32(2 * TOK_DEV)
        return row_loss, gimg_own + gimg_prev, gtxt_own, gtxt_prev

    row_loss, grad_img, gtxt_own, gtxt_prev = lax.map(one_block, (image_blocks, text_blocks, prev_blocks, partner_blocks, block_ids))
    grad_txt = gtxt_own + jnp.roll(gtxt_prev, -1, axis=0)
    return (row_loss.reshape(TOKENS), grad_img.reshape(TOKENS, D).astype(jnp.bfloat16), grad_txt.reshape(TOKENS, D).astype(jnp.bfloat16))
```

```python
import functools
import jax
import jax.numpy as jnp
from jax import lax
from jax.experimental import pallas as pl
from jax.experimental.pallas import tpu as pltpu
from jax.sharding import PartitionSpec as P

AXES = ("dp", "rep")
NT = (((1,), (1,)), ((), ()))
TN = (((0,), (0,)), ((), ()))


def place(flat):
    dp, rep = divmod(flat, 4)
    return dp // 8, (rep // 2) * 2 + (dp // 4) % 2, dp % 4, rep % 2


def flat_of(y, x, z, core):
    return (y * 8 + (x % 2) * 4 + z) * 4 + (x // 2) * 2 + core


def moved(x=0, z=0, core=0):
    route = []
    for source in range(128):
        sy, sx, sz, sc = place(source)
        route.append((source, flat_of(sy, (sx + x) % 4, (sz + z) % 4, (sc + core) % 2)))
    return route


def along_loop(step):
    return [(source, (source + 4 * step) % 128) for source in range(128)]


def send(block, route):
    return lax.ppermute(block, AXES, route)


def shifted(block, step, head):
    along_z = dict(moved(z=step))
    turn = 3 if step > 0 else 0
    hop = [(along_z[s], d) for s, d in along_loop(step) if place(s)[2] == turn]
    first = send(block[:head], moved(z=step))
    rest = send(block[head:], along_loop(step))
    turned = send(first, hop)
    here = lax.axis_index("dp") % 4 == (turn + step) % 4
    return jnp.concatenate([jnp.where(here, turned, first), rest])


def terms(dots, positive, temper, shift):
    logit = temper * dots + shift
    z = jnp.where(positive, -logit, logit)
    e = jnp.exp(-jnp.abs(z))
    log_term = jnp.where(e < 1e-4, e, jnp.log(1.0 + e))
    loss = jnp.maximum(z, 0.0) + log_term
    sigmoid = jnp.exp(jnp.minimum(z, 0.0) - log_term)
    coef = (jnp.where(positive, -temper, temper) * sigmoid).astype(jnp.bfloat16)
    return loss, coef


def pair_body(n, has_gi, has_gt, tile, start_ref, scale_ref, offset_ref, *refs):
    imgs, parts, txt, refs = refs[:n], refs[n : 2 * n], refs[2 * n], refs[2 * n + 1 :]
    if has_gi:
        gi_in, loss_in, refs = refs[:n], refs[n : 2 * n], refs[2 * n :]
    if has_gt:
        gt_in, refs = refs[0], refs[1:]
    gi, loss, gt = refs[:n], refs[n : 2 * n], refs[2 * n]
    step = pl.program_id(0)
    temper, shift = scale_ref[0], offset_ref[0]

    @pl.when(step == 0)
    def _():
        for m in range(n):
            if has_gi:
                gi[m][...] = gi_in[m][...]
                loss[m][...] = loss_in[m][...]
            else:
                gi[m][...] = jnp.zeros_like(gi[m])
                loss[m][...] = jnp.zeros_like(loss[m])

    t = txt[...]
    rows = imgs[0].shape[0]
    col = start_ref[0] + step * tile + lax.broadcasted_iota(jnp.int32, (tile, rows), 0)
    acc = gt_in[...].astype(jnp.float32) if has_gt else None
    for m in range(n):
        a = imgs[m][...]
        dots = lax.dot_general(t, a, NT, preferred_element_type=jnp.float32)
        ls, coef = terms(dots, parts[m][...] == col, temper, shift)
        loss[m][...] += jnp.sum(ls, axis=0, keepdims=True)
        gi[m][...] += lax.dot_general(coef, t, TN, preferred_element_type=jnp.float32)
        g = jnp.dot(coef, a, preferred_element_type=jnp.float32)
        acc = g if acc is None else acc + g
    gt[...] = acc.astype(gt.dtype)


def pairs(imgs, parts, txt, start, scale, offset, gi=None, loss=None, gt=None, gt_dtype=jnp.float32, tile=512):
    n, (rows, d), nt = len(imgs), imgs[0].shape, txt.shape[0]
    smem = pl.BlockSpec(memory_space=pltpu.SMEM)
    tiled = pl.BlockSpec((tile, d), lambda i: (i, 0))

    def whole(r, c):
        return pl.BlockSpec((r, c), lambda i: (0, 0))

    in_specs = [smem] * 3 + [whole(rows, d)] * n + [whole(1, rows)] * n + [tiled]
    args = [start.astype(jnp.int32)[None], scale, offset, *imgs, *parts, txt]
    if gi is not None:
        in_specs += [whole(rows, d)] * n + [whole(1, rows)] * n
        args += [*gi, *loss]
    if gt is not None:
        in_specs += [tiled]
        args += [gt]
    outs = pl.pallas_call(
        functools.partial(pair_body, n, gi is not None, gt is not None, tile),
        grid=(nt // tile,),
        in_specs=in_specs,
        out_specs=[whole(rows, d)] * n + [whole(1, rows)] * n + [tiled],
        out_shape=[jax.ShapeDtypeStruct((rows, d), jnp.float32)] * n
        + [jax.ShapeDtypeStruct((1, rows), jnp.float32)] * n
        + [jax.ShapeDtypeStruct((nt, d), gt_dtype)],
        compiler_params=pltpu.CompilerParams(vmem_limit_bytes=48 << 20),
        cost_estimate=pl.CostEstimate(
            flops=6 * n * rows * nt * d, bytes_accessed=nt * d * 8 + n * rows * d * 8, transcendentals=3 * n * rows * nt
        ),
    )(*args)
    return outs[:n], outs[n : 2 * n], outs[2 * n]


def body(images, texts, partner, scale, offset):
    dp, rep = lax.axis_index("dp"), lax.axis_index("rep")
    rows = texts.shape[0]

    def start(other_chip, other_core):
        c, b = rep // 2, rep % 2
        return (dp * 4 + (c ^ other_chip) * 2 + (b ^ other_core)) * rows

    swap = moved(core=1)
    across = moved(x=2)
    near_far = send(texts, swap)
    visitor = shifted(images, -1, 256)
    far = send(texts, across)
    visitor_partner = send(partner, along_loop(-1))
    far_far = send(far, swap)
    pa, pb = partner[None, :], visitor_partner[None, :]
    (ga,), (la,), gs = pairs([images], [pa], texts, start(0, 0), scale, offset)
    (ga,), (la,), gs_far = pairs([images], [pa], near_far, start(0, 1), scale, offset, [ga], [la])
    (gb,), (lb,), gs = pairs([visitor], [pb], texts, start(0, 0), scale, offset, gt=gs)
    (gb,), (lb,), gs_far = pairs([visitor], [pb], near_far, start(0, 1), scale, offset, [gb], [lb], gt=gs_far)
    (ga, gb), (la, lb), gu_far = pairs(
        [images, visitor], [pa, pb], far_far, start(1, 1), scale, offset, [ga, gb], [la, lb], gt_dtype=jnp.bfloat16
    )
    gu_got = send(gu_far, swap)
    (ga, gb), (la, lb), gu = pairs(
        [images, visitor], [pa, pb], far, start(1, 0), scale, offset, [ga, gb], [la, lb], gt=gu_got
    )
    back = shifted(gb.astype(jnp.bfloat16), 1, 256)
    back_loss = send(lb[0], along_loop(1))
    gu_back = send(gu.astype(jnp.bfloat16), across)
    gs_got = send(gs_far, swap)
    row_loss = (la[0] + back_loss) / jnp.float32(8 * rows)
    grad_images = (ga + back.astype(jnp.float32)).astype(jnp.bfloat16)
    grad_texts = (gs + gs_got + gu_back.astype(jnp.float32)).astype(jnp.bfloat16)
    return row_loss, grad_images, grad_texts


def solution(mesh):
    in_specs = (P(AXES, None), P(AXES, None), P(AXES), P(), P())
    out_specs = (P(AXES), P(AXES, None), P(AXES, None))
    return jax.shard_map(body, mesh=mesh, in_specs=in_specs, out_specs=out_specs, check_vma=False)
```

```python
import functools
import jax
import jax.numpy as jnp
from jax import lax
from jax.experimental import pallas as pl
from jax.experimental.pallas import tpu as pltpu
from jax.sharding import PartitionSpec as P

AXES = ("dp", "rep")
NT = (((1,), (1,)), ((), ()))
TN = (((0,), (0,)), ((), ()))
F32, BF16 = jnp.float32, jnp.bfloat16


def place(flat):
    dp, rep = divmod(flat, 4)
    return dp // 8, (rep // 2) * 2 + (dp // 4) % 2, dp % 4, rep % 2


def flat_of(y, x, z, core):
    return (y * 8 + (x % 2) * 4 + z) * 4 + (x // 2) * 2 + core


def moved(x=0, z=0, core=0):
    route = []
    for source in range(128):
        sy, sx, sz, sc = place(source)
        route.append((source, flat_of(sy, (sx + x) % 4, (sz + z) % 4, (sc + core) % 2)))
    return route


def along_loop(step, core=0):
    return [(source, ((source + 4 * step) % 128) ^ core) for source in range(128)]


def last_hop(step):
    along_z = dict(moved(z=step))
    turn = 3 if step > 0 else 0
    return [(along_z[s], d) for s, d in along_loop(step) if place(s)[2] == turn]


def send(block, route):
    return lax.ppermute(block, AXES, route)


def after(block, *others):
    return lax.optimization_barrier((block, *others))[0]


def terms(dots, positive, temper, shift):
    logit = temper * dots + shift
    z = jnp.where(positive, -logit, logit)
    e = jnp.exp(-jnp.abs(z))
    log_term = jnp.where(e < 1e-4, e, jnp.log(1.0 + e))
    loss = jnp.maximum(z, 0.0) + log_term
    sigmoid = jnp.exp(jnp.minimum(z, 0.0) - log_term)
    coef = (jnp.where(positive, -temper, temper) * sigmoid).astype(BF16)
    return loss, coef


SMEM = pl.BlockSpec(memory_space=pltpu.SMEM)
VMEM = pl.BlockSpec(memory_space=pltpu.VMEM)
ROWS, WIDTH, HALF = 512, 1152, 256
CARRY = 16


def near(array):
    return pltpu.with_memory_space_constraint(array, pltpu.VMEM)


def call(kernel, smalls, arrays, outs, alias=None, cells=0):
    return pl.pallas_call(
        kernel,
        in_specs=[SMEM] * len(smalls) + [VMEM] * len(arrays),
        out_specs=[VMEM] * len(outs),
        out_shape=outs,
        input_output_aliases=alias or {},
        compiler_params=pltpu.CompilerParams(vmem_limit_bytes=16 << 20),
        cost_estimate=pl.CostEstimate(flops=1000, bytes_accessed=1000, transcendentals=0),
    )(*smalls, *map(near, arrays))


def split3(value):
    high = value.astype(BF16)
    middle = (value - high.astype(F32)).astype(BF16)
    low = (value - high.astype(F32) - middle.astype(F32)).astype(BF16)
    return high, middle, low


def put_loss(ref, at, loss):
    if ref.dtype == F32:
        ref[pl.ds(at, 8), :ROWS] = jnp.broadcast_to(loss, (8, ROWS))
        return
    row = lax.broadcasted_iota(jnp.int32, (CARRY, ROWS), 0)
    parts = [part.astype(F32) for part in split3(loss)]
    block = jnp.where(row == 0, parts[0], jnp.where(row == 1, parts[1], jnp.where(row == 2, parts[2], 0.0)))
    ref[pl.ds(at, CARRY), :ROWS] = block.astype(BF16)


def get_loss(ref, at):
    if ref.dtype == F32:
        return ref[pl.ds(at, 8), :ROWS][0:1]
    parts = ref[pl.ds(at, CARRY), :ROWS].astype(F32)
    return parts[0:1] + parts[1:2] + parts[2:3]


def pair_body(gi_has, gt_has, start_ref, scale_ref, offset_ref, *refs):
    refs = list(refs)

    def take(count):
        out = refs[:count]
        del refs[:count]
        return out

    imgs, txt = take(2), take(1)[0]
    gi_in = take(2) if gi_has else None
    gt_in = take(1)[0] if gt_has else None
    gi, gt = take(2), take(1)[0]
    temper, shift = scale_ref[0], offset_ref[0]
    t = txt[...]
    col = start_ref[0] + lax.broadcasted_iota(jnp.int32, (ROWS, ROWS), 0).astype(F32)
    t_sum = gt_in[...] if gt_has else None
    for m in range(2):
        a = imgs[m][:ROWS, :]
        code = imgs[m][pl.ds(ROWS, CARRY), :ROWS].astype(F32)
        partner = code[0:1] * 256.0 + code[1:2]
        dots = lax.dot_general(t, a, NT, preferred_element_type=F32)
        ls, coef = terms(dots, partner == col, temper, shift)
        loss = jnp.sum(ls, axis=0, keepdims=True)
        g = lax.dot_general(coef, t, TN, preferred_element_type=F32)
        d = jnp.dot(coef, a, preferred_element_type=F32)
        if gi_has:
            loss = loss + get_loss(gi_in[m], ROWS)
            g = g + gi_in[m][:ROWS, :]
        gi[m][:ROWS, :] = g.astype(gi[m].dtype)
        put_loss(gi[m], ROWS, loss)
        t_sum = d if t_sum is None else t_sum + d
    gt[...] = t_sum.astype(gt.dtype)


def grad_shape(ty):
    return pltpu.VMEM((ROWS + (8 if ty == F32 else CARRY), WIDTH), ty)


def pairs(imgs, txt, start, scale, offset, gi=None, gt=None, gi_types=(F32, F32), gt_type=F32):
    arrays = [*imgs, txt, *(gi or []), *([gt] if gt is not None else [])]
    alias = {}
    if gi is not None:
        alias.update({6 + m: m for m in range(2) if gi_types[m] == F32})
    if gt is not None and gt_type == F32:
        alias[5 + len(arrays) - 3] = 2
    outs = [grad_shape(ty) for ty in gi_types] + [pltpu.VMEM((ROWS, WIDTH), gt_type)]
    got = call(
        functools.partial(pair_body, gi is not None, gt is not None), (start, scale, offset), arrays, outs, alias
    )
    return got[:2], got[2]


def assemble_body(flag_ref, first, turned, rest, out):
    out[:HALF, :] = jnp.where(flag_ref[0] == 1, turned[...], first[...])
    out[HALF:, :] = rest[...]


def fold_body(mine, other, top, rest):
    top[...] = (mine[:HALF, :] + other[:HALF, :].astype(F32)).astype(BF16)
    rest[:HALF, :] = (mine[HALF:ROWS, :] + other[HALF:ROWS, :].astype(F32)).astype(BF16)
    put_loss(rest, HALF, get_loss(mine, ROWS) + get_loss(other, ROWS))


def image_body(flag_ref, mine, other, first, turned, rest, grad, row_loss):
    top = jnp.where(flag_ref[0] == 1, turned[...], first[...]).astype(F32)
    grad[:HALF, :] = (mine[:HALF, :] + other[:HALF, :] + top).astype(BF16)
    below = rest[:HALF, :].astype(F32)
    grad[HALF:, :] = (mine[HALF:ROWS, :] + other[HALF:ROWS, :] + below).astype(BF16)
    loss = get_loss(mine, ROWS) + get_loss(other, ROWS) + get_loss(rest, HALF)
    row_loss[...] = loss / (8.0 * ROWS)


def add_body(one, two, out):
    out[...] = one[...] + two[...]


def text_body(mine, back, grad):
    grad[...] = (mine[...] + back[...].astype(F32)).astype(BF16)


def body(images, texts, partner, scale, offset):
    dp, rep = lax.axis_index("dp"), lax.axis_index("rep")
    start = ((dp * 4 + rep) * ROWS).astype(F32)[None]
    far_start = ((dp * 4 + (rep ^ 2)) * ROWS).astype(F32)[None]
    swap = moved(core=1)
    across = moved(x=2)

    def flag(z):
        return (dp % 4 == z).astype(jnp.int32)[None]

    code = jnp.stack([partner // 256, partner % 256]).astype(BF16)
    own = jnp.concatenate([images, jnp.pad(code, ((0, CARRY - 2), (0, WIDTH - ROWS)))])
    far = send(texts, across)
    first = send(images[:HALF], moved(z=-1))
    own2 = send(own, swap)
    (ga, ga2), gs = pairs([own, own2], texts, start, scale, offset)
    turned = send(after(first, gs), last_hop(-1))
    rest = send(after(own[HALF:], far, gs), along_loop(-1))
    (ga, ga2), gu = pairs([own, own2], far, far_start, scale, offset, [ga, ga2])
    visitor = call(
        assemble_body, (flag(3),), (after(first, gu), turned, rest), [pltpu.VMEM((ROWS + CARRY, WIDTH), BF16)]
    )[0]
    visitor2 = send(visitor, swap)
    (gb, gb2), gs2 = pairs([visitor, visitor2], texts, start, scale, offset)
    (gb, gb2), gu = pairs([visitor, visitor2], far, far_start, scale, offset, [gb, gb2], gu, (F32, BF16), BF16)
    gu_back = send(gu, across)
    gb_got = send(gb2, swap)
    top, bottom = call(
        fold_body, (), (gb, gb_got),
        [pltpu.VMEM((HALF, WIDTH), BF16), pltpu.VMEM((HALF + CARRY, WIDTH), BF16)],
    )
    back_first = send(top, moved(z=1))
    back_rest = send(after(bottom, back_first), along_loop(1))
    gs = call(add_body, (), (after(gs, top), gs2), [pltpu.VMEM((ROWS, WIDTH), F32)], {0: 0})[0]
    back_turned = send(back_first, last_hop(1))
    ga_got = send(after(ga2, top), swap)
    grad_texts = call(text_body, (), (gs, gu_back), [jax.ShapeDtypeStruct((ROWS, WIDTH), BF16)])[0]
    grad_images, row_loss = call(
        image_body, (flag(0),), (ga, ga_got, back_first, back_turned, back_rest),
        [jax.ShapeDtypeStruct((ROWS, WIDTH), BF16), jax.ShapeDtypeStruct((1, ROWS), F32)],
    )
    return row_loss[0], grad_images, grad_texts


def solution(mesh):
    in_specs = (P(AXES, None), P(AXES, None), P(AXES), P(), P())
    out_specs = (P(AXES), P(AXES, None), P(AXES, None))
    return jax.shard_map(body, mesh=mesh, in_specs=in_specs, out_specs=out_specs, check_vma=False)
```

```python
import functools
import jax
import jax.numpy as jnp
from jax import lax
from jax.experimental import pallas as pl
from jax.experimental.pallas import tpu as pltpu
from jax.sharding import PartitionSpec as P

AXES = ("dp", "rep")
NT = (((1,), (1,)), ((), ()))
TN = (((0,), (0,)), ((), ()))
F32, BF16 = jnp.float32, jnp.bfloat16


def place(flat):
    dp, rep = divmod(flat, 4)
    return dp // 8, (rep // 2) * 2 + (dp // 4) % 2, dp % 4, rep % 2


def flat_of(y, x, z, core):
    return (y * 8 + (x % 2) * 4 + z) * 4 + (x // 2) * 2 + core


def moved(x=0, z=0, core=0):
    route = []
    for source in range(128):
        sy, sx, sz, sc = place(source)
        route.append((source, flat_of(sy, (sx + x) % 4, (sz + z) % 4, (sc + core) % 2)))
    return route


def along_loop(step, core=0):
    return [(source, ((source + 4 * step) % 128) ^ core) for source in range(128)]


def last_hop(step):
    along_z = dict(moved(z=step))
    turn = 3 if step > 0 else 0
    return [(along_z[s], d) for s, d in along_loop(step) if place(s)[2] == turn]


def send(block, route):
    return lax.ppermute(block, AXES, route)


def after(block, *others):
    return lax.optimization_barrier((block, *others))[0]


def terms(dots, positive, temper, shift):
    logit = temper * dots + shift
    z = jnp.where(positive, -logit, logit)
    e = jnp.exp(-jnp.abs(z))
    log_term = jnp.where(e < 1e-4, e, jnp.log(1.0 + e))
    loss = jnp.maximum(z, 0.0) + log_term
    sigmoid = jnp.exp(jnp.minimum(z, 0.0) - log_term)
    coef = (jnp.where(positive, -temper, temper) * sigmoid).astype(BF16)
    return loss, coef


SMEM = pl.BlockSpec(memory_space=pltpu.SMEM)
VMEM = pl.BlockSpec(memory_space=pltpu.VMEM)
ROWS, WIDTH, HALF = 512, 1152, 256
FIRST = 256
CARRY = 16


def near(array):
    return pltpu.with_memory_space_constraint(array, pltpu.VMEM)


def call(kernel, smalls, arrays, outs, alias=None, cells=0):
    return pl.pallas_call(
        kernel,
        in_specs=[SMEM] * len(smalls) + [VMEM] * len(arrays),
        out_specs=[VMEM] * len(outs),
        out_shape=outs,
        input_output_aliases=alias or {},
        compiler_params=pltpu.CompilerParams(vmem_limit_bytes=16 << 20),
        cost_estimate=pl.CostEstimate(flops=1000, bytes_accessed=1000, transcendentals=0),
    )(*smalls, *map(near, arrays))


def split3(value):
    high = value.astype(BF16)
    middle = (value - high.astype(F32)).astype(BF16)
    low = (value - high.astype(F32) - middle.astype(F32)).astype(BF16)
    return high, middle, low


def put_loss(ref, at, loss):
    if ref.dtype == F32:
        ref[pl.ds(at, 8), :ROWS] = jnp.broadcast_to(loss, (8, ROWS))
        return
    row = lax.broadcasted_iota(jnp.int32, (CARRY, ROWS), 0)
    parts = [part.astype(F32) for part in split3(loss)]
    block = jnp.where(row == 0, parts[0], jnp.where(row == 1, parts[1], jnp.where(row == 2, parts[2], 0.0)))
    ref[pl.ds(at, CARRY), :ROWS] = block.astype(BF16)


def get_loss(ref, at):
    if ref.dtype == F32:
        return ref[pl.ds(at, 8), :ROWS][0:1]
    parts = ref[pl.ds(at, CARRY), :ROWS].astype(F32)
    return parts[0:1] + parts[1:2] + parts[2:3]


def pair_body(n, gi_has, gt_has, start_ref, scale_ref, offset_ref, *refs):
    refs = list(refs)

    def take(count):
        out = refs[:count]
        del refs[:count]
        return out

    imgs, txt = take(n), take(1)[0]
    gi_in = take(n) if gi_has else None
    gt_in = take(1)[0] if gt_has else None
    gi, gt = take(n), take(1)[0]
    temper, shift = scale_ref[0], offset_ref[0]
    t = txt[...]
    col = start_ref[0] + lax.broadcasted_iota(jnp.int32, (t.shape[0], ROWS), 0).astype(F32)
    t_sum = None
    for m in range(n):
        a = imgs[m][:ROWS, :]
        code = imgs[m][pl.ds(ROWS, CARRY), :ROWS].astype(F32)
        partner = code[0:1] * 256.0 + code[1:2]
        dots = lax.dot_general(t, a, NT, preferred_element_type=F32)
        ls, coef = terms(dots, partner == col, temper, shift)
        loss = jnp.sum(ls, axis=0, keepdims=True)
        g = lax.dot_general(coef, t, TN, preferred_element_type=F32)
        d = jnp.dot(coef, a, preferred_element_type=F32)
        if gi_has:
            loss = loss + get_loss(gi_in[m], ROWS)
            g = g + gi_in[m][:ROWS, :]
        gi[m][:ROWS, :] = g.astype(gi[m].dtype)
        put_loss(gi[m], ROWS, loss)
        t_sum = d if t_sum is None else t_sum + d
    if gt_has:
        t_sum = t_sum + gt_in[...]
    gt[...] = t_sum.astype(gt.dtype)


def grad_shape(ty):
    return pltpu.VMEM((ROWS + (8 if ty == F32 else CARRY), WIDTH), ty)


def pairs(imgs, txt, start, scale, offset, gi=None, gi_types=None, gt=None, gt_type=F32):
    n = len(imgs)
    gi_types = gi_types or [F32] * n
    alias = {4 + n + m: m for m in range(n) if gi is not None and gi_types[m] == F32}
    outs = [grad_shape(ty) for ty in gi_types] + [pltpu.VMEM(txt.shape, gt_type)]
    got = call(
        functools.partial(pair_body, n, gi is not None, gt is not None),
        (start, scale, offset),
        [*imgs, txt, *(gi or []), *([gt] if gt is not None else [])],
        outs,
        alias,
    )
    return got[:n], got[n]


def assemble_body(flag_ref, first, turned, rest, out):
    out[:HALF, :] = jnp.where(flag_ref[0] == 1, turned[...], first[...])
    out[HALF:, :] = rest[...]


def fold_body(mine, other, top, rest):
    top[...] = (mine[:HALF, :] + other[:HALF, :].astype(F32)).astype(BF16)
    rest[:HALF, :] = (mine[HALF:ROWS, :] + other[HALF:ROWS, :].astype(F32)).astype(BF16)
    put_loss(rest, HALF, get_loss(mine, ROWS) + get_loss(other, ROWS))


def image_body(flag_ref, mine, first, turned, rest, grad, row_loss):
    top = jnp.where(flag_ref[0] == 1, turned[...], first[...]).astype(F32)
    grad[:HALF, :] = (mine[:HALF, :] + top).astype(BF16)
    grad[HALF:, :] = (mine[HALF:ROWS, :] + rest[:HALF, :].astype(F32)).astype(BF16)
    loss = get_loss(mine, ROWS) + get_loss(rest, HALF)
    row_loss[...] = loss / (8.0 * ROWS)


def add_body(one, two, out):
    out[...] = one[...] + two[...]


def text_body(mine, back1, back2, grad):
    grad[:FIRST, :] = (mine[:FIRST, :] + back1[...].astype(F32)).astype(BF16)
    grad[FIRST:, :] = (mine[FIRST:, :] + back2[...].astype(F32)).astype(BF16)


def body(images, texts, partner, scale, offset):
    dp, rep = lax.axis_index("dp"), lax.axis_index("rep")
    start = ((dp * 4 + rep) * ROWS).astype(F32)[None]
    far_start = ((dp * 4 + (rep ^ 2)) * ROWS).astype(F32)[None]
    swap = moved(core=1)
    across = moved(x=2)

    def flag(z):
        return (dp % 4 == z).astype(jnp.int32)[None]

    code = jnp.stack([partner // 256, partner % 256]).astype(BF16)
    own = jnp.concatenate([images, jnp.pad(code, ((0, CARRY - 2), (0, WIDTH - ROWS)))])
    far1 = send(texts[:FIRST], across)
    first = send(images[:HALF], moved(z=-1))
    own2 = send(own, swap)
    (ga, ga2), gs = pairs([own, own2], texts, start, scale, offset)
    rest = send(after(own[HALF:], first, gs, far1), along_loop(-1))
    turned = send(after(first, gs, far1), last_hop(-1))
    (ga, ga2), gu = pairs([own, own2], far1, far_start, scale, offset, [ga, ga2])
    far2 = send(after(texts[FIRST:], far1), across)
    visitor = call(
        assemble_body, (flag(3),), (after(first, gu), turned, rest), [pltpu.VMEM((ROWS + CARRY, WIDTH), BF16)]
    )[0]
    visitor2 = send(visitor, swap)
    (gb, gb2), gs2 = pairs([visitor, visitor2], texts, start, scale, offset)
    (gb, gb2), gu = pairs([visitor, visitor2], far1, far_start, scale, offset, [gb, gb2], None, gu, BF16)
    every = [own, own2, visitor, visitor2]
    gu1_back = send(gu, across)
    (ga, ga2, gb, gb2), gu2 = pairs(
        every, far2, far_start + FIRST, scale, offset, [ga, ga2, gb, gb2], [F32, F32, F32, BF16], None, BF16
    )
    gu2_back = send(gu2, across)
    gb_got = send(after(gb2, gu1_back), swap)
    top, bottom = call(
        fold_body, (), (gb, gb_got),
        [pltpu.VMEM((HALF, WIDTH), BF16), pltpu.VMEM((HALF + CARRY, WIDTH), BF16)],
    )
    back_first = send(top, moved(z=1))
    back_rest = send(after(bottom, back_first, gu2_back), along_loop(1))
    gs = call(add_body, (), (after(gs, top), gs2), [pltpu.VMEM((ROWS, WIDTH), F32)], {0: 0})[0]
    back_turned = send(after(back_first, gu2_back), last_hop(1))
    ga_got = send(after(ga2, top), swap)
    ga = call(add_body, (), (ga, ga_got), [grad_shape(F32)], {0: 0})[0]
    grad_texts = call(text_body, (), (gs, gu1_back, gu2_back), [jax.ShapeDtypeStruct((ROWS, WIDTH), BF16)])[0]
    grad_images, row_loss = call(
        image_body, (flag(0),), (ga, back_first, back_turned, back_rest),
        [jax.ShapeDtypeStruct((ROWS, WIDTH), BF16), jax.ShapeDtypeStruct((1, ROWS), F32)],
    )
    return row_loss[0], grad_images, grad_texts


def solution(mesh):
    in_specs = (P(AXES, None), P(AXES, None), P(AXES), P(), P())
    out_specs = (P(AXES), P(AXES, None), P(AXES, None))
    return jax.shard_map(body, mesh=mesh, in_specs=in_specs, out_specs=out_specs, check_vma=False)
```

```python
import functools
import jax
import jax.numpy as jnp
from jax import lax
from jax.experimental import pallas as pl
from jax.experimental.pallas import tpu as pltpu
from jax.sharding import PartitionSpec as P

AXES = ("dp", "rep")
NT = (((1,), (1,)), ((), ()))
TN = (((0,), (0,)), ((), ()))
F32, BF16 = jnp.float32, jnp.bfloat16


def place(flat):
    dp, rep = divmod(flat, 4)
    return dp // 8, (rep // 2) * 2 + (dp // 4) % 2, dp % 4, rep % 2


def flat_of(y, x, z, core):
    return (y * 8 + (x % 2) * 4 + z) * 4 + (x // 2) * 2 + core


def moved(x=0, z=0, core=0):
    route = []
    for source in range(128):
        sy, sx, sz, sc = place(source)
        route.append((source, flat_of(sy, (sx + x) % 4, (sz + z) % 4, (sc + core) % 2)))
    return route


def along_loop(step, core=0):
    return [(source, ((source + 4 * step) % 128) ^ core) for source in range(128)]


def last_hop(step):
    along_z = dict(moved(z=step))
    turn = 3 if step > 0 else 0
    return [(along_z[s], d) for s, d in along_loop(step) if place(s)[2] == turn]


def send(block, route):
    return lax.ppermute(block, AXES, route)


def after(block, *others):
    return lax.optimization_barrier((block, *others))[0]


def terms(dots, positive, temper, shift):
    logit = temper * dots + shift
    z = jnp.where(positive, -logit, logit)
    e = jnp.exp(-jnp.abs(z))
    log_term = jnp.where(e < 1e-4, (1.0 - 0.5 * e) * e, jnp.log(1.0 + e))
    loss = jnp.maximum(z, 0.0) + log_term
    sigmoid = jnp.exp(jnp.minimum(z, 0.0) - log_term)
    coef = (jnp.where(positive, -temper, temper) * sigmoid).astype(BF16)
    return loss, coef


SMEM = pl.BlockSpec(memory_space=pltpu.SMEM)
VMEM = pl.BlockSpec(memory_space=pltpu.VMEM)
ROWS, WIDTH, HALF = 512, 1152, 256
FIRST = 256
CARRY = 16


def near(array):
    return pltpu.with_memory_space_constraint(array, pltpu.VMEM)


def call(kernel, smalls, arrays, outs, alias=None, cells=0):
    return pl.pallas_call(
        kernel,
        in_specs=[SMEM] * len(smalls) + [VMEM] * len(arrays),
        out_specs=[VMEM] * len(outs),
        out_shape=outs,
        input_output_aliases=alias or {},
        compiler_params=pltpu.CompilerParams(vmem_limit_bytes=16 << 20),
        cost_estimate=pl.CostEstimate(flops=1000, bytes_accessed=1000, transcendentals=0),
    )(*smalls, *map(near, arrays))


def split3(value):
    high = value.astype(BF16)
    middle = (value - high.astype(F32)).astype(BF16)
    low = (value - high.astype(F32) - middle.astype(F32)).astype(BF16)
    return high, middle, low


def put_loss(ref, at, loss):
    if ref.dtype == F32:
        ref[pl.ds(at, 8), :ROWS] = jnp.broadcast_to(loss, (8, ROWS))
        return
    row = lax.broadcasted_iota(jnp.int32, (CARRY, ROWS), 0)
    parts = [part.astype(F32) for part in split3(loss)]
    block = jnp.where(row == 0, parts[0], jnp.where(row == 1, parts[1], jnp.where(row == 2, parts[2], 0.0)))
    ref[pl.ds(at, CARRY), :ROWS] = block.astype(BF16)


def get_loss(ref, at):
    if ref.dtype == F32:
        return ref[pl.ds(at, 8), :ROWS][0:1]
    parts = ref[pl.ds(at, CARRY), :ROWS].astype(F32)
    return parts[0:1] + parts[1:2] + parts[2:3]


def pair_body(n, gi_has, gt_has, start_ref, scale_ref, offset_ref, *refs):
    refs = list(refs)

    def take(count):
        out = refs[:count]
        del refs[:count]
        return out

    imgs, txt = take(n), take(1)[0]
    gi_in = take(n) if gi_has else None
    gt_in = take(1)[0] if gt_has else None
    gi, gt = take(n), take(1)[0]
    temper, shift = scale_ref[0], offset_ref[0]
    t = txt[...]
    col = start_ref[0] + lax.broadcasted_iota(jnp.int32, (t.shape[0], ROWS), 0).astype(F32)
    t_sum = None
    for m in range(n):
        a = imgs[m][:ROWS, :]
        code = imgs[m][pl.ds(ROWS, CARRY), :ROWS].astype(F32)
        partner = code[0:1] * 256.0 + code[1:2]
        dots = lax.dot_general(t, a, NT, preferred_element_type=F32)
        ls, coef = terms(dots, partner == col, temper, shift)
        loss = jnp.sum(ls, axis=0, keepdims=True)
        g = lax.dot_general(coef, t, TN, preferred_element_type=F32)
        d = jnp.dot(coef, a, preferred_element_type=F32)
        if gi_has:
            loss = loss + get_loss(gi_in[m], ROWS)
            g = g + gi_in[m][:ROWS, :]
        gi[m][:ROWS, :] = g.astype(gi[m].dtype)
        put_loss(gi[m], ROWS, loss)
        t_sum = d if t_sum is None else t_sum + d
    if gt_has:
        t_sum = t_sum + gt_in[...]
    gt[...] = t_sum.astype(gt.dtype)


def grad_shape(ty):
    return pltpu.VMEM((ROWS + (8 if ty == F32 else CARRY), WIDTH), ty)


def pairs(imgs, txt, start, scale, offset, gi=None, gi_types=None, gt=None, gt_type=F32):
    n = len(imgs)
    gi_types = gi_types or [F32] * n
    alias = {4 + n + m: m for m in range(n) if gi is not None and gi_types[m] == F32}
    outs = [grad_shape(ty) for ty in gi_types] + [pltpu.VMEM(txt.shape, gt_type)]
    got = call(
        functools.partial(pair_body, n, gi is not None, gt is not None),
        (start, scale, offset),
        [*imgs, txt, *(gi or []), *([gt] if gt is not None else [])],
        outs,
        alias,
    )
    return got[:n], got[n]


def assemble_body(flag_ref, first, turned, rest, out):
    out[:HALF, :] = jnp.where(flag_ref[0] == 1, turned[...], first[...])
    out[HALF:, :] = rest[...]


def fold_body(mine, other, top, rest):
    top[...] = (mine[:HALF, :] + other[:HALF, :].astype(F32)).astype(BF16)
    rest[:HALF, :] = (mine[HALF:ROWS, :] + other[HALF:ROWS, :].astype(F32)).astype(BF16)
    put_loss(rest, HALF, get_loss(mine, ROWS) + get_loss(other, ROWS))


def image_body(flag_ref, mine, first, turned, rest, grad, row_loss):
    top = jnp.where(flag_ref[0] == 1, turned[...], first[...]).astype(F32)
    grad[:HALF, :] = (mine[:HALF, :] + top).astype(BF16)
    grad[HALF:, :] = (mine[HALF:ROWS, :] + rest[:HALF, :].astype(F32)).astype(BF16)
    loss = get_loss(mine, ROWS) + get_loss(rest, HALF)
    row_loss[...] = loss / (8.0 * ROWS)


def add_body(one, two, out):
    out[...] = one[...] + two[...]


def text_body(mine, back1, back2, grad):
    grad[:FIRST, :] = (mine[:FIRST, :] + back1[...].astype(F32)).astype(BF16)
    grad[FIRST:, :] = (mine[FIRST:, :] + back2[...].astype(F32)).astype(BF16)


def body(images, texts, partner, scale, offset):
    dp, rep = lax.axis_index("dp"), lax.axis_index("rep")
    start = ((dp * 4 + rep) * ROWS).astype(F32)[None]
    far_start = ((dp * 4 + (rep ^ 2)) * ROWS).astype(F32)[None]
    swap = moved(core=1)
    across = moved(x=2)

    def flag(z):
        return (dp % 4 == z).astype(jnp.int32)[None]

    code = jnp.stack([partner // 256, partner % 256]).astype(BF16)
    own = jnp.concatenate([images, jnp.pad(code, ((0, CARRY - 2), (0, WIDTH - ROWS)))])
    far1 = send(texts[:FIRST], across)
    first = send(images[:HALF], moved(z=-1))
    own2 = send(own, swap)
    (ga, ga2), gs = pairs([own, own2], texts, start, scale, offset)
    rest = send(after(own[HALF:], first, gs, far1), along_loop(-1))
    turned = send(after(first, gs, far1), last_hop(-1))
    (ga, ga2), gu = pairs([own, own2], far1, far_start, scale, offset, [ga, ga2])
    far2 = send(after(texts[FIRST:], far1), across)
    visitor = call(
        assemble_body, (flag(3),), (after(first, gu), turned, rest), [pltpu.VMEM((ROWS + CARRY, WIDTH), BF16)]
    )[0]
    visitor2 = send(visitor, swap)
    (gb, gb2), gs2 = pairs([visitor, visitor2], texts, start, scale, offset)
    (gb, gb2), gu = pairs([visitor, visitor2], far1, far_start, scale, offset, [gb, gb2], None, gu, BF16)
    every = [own, own2, visitor, visitor2]
    gu1_back = send(gu, across)
    (ga, ga2, gb, gb2), gu2 = pairs(
        every, far2, far_start + FIRST, scale, offset, [ga, ga2, gb, gb2], [F32, F32, F32, BF16], None, BF16
    )
    gu2_back = send(gu2, across)
    gb_got = send(after(gb2, gu1_back), swap)
    top, bottom = call(
        fold_body, (), (gb, gb_got),
        [pltpu.VMEM((HALF, WIDTH), BF16), pltpu.VMEM((HALF + CARRY, WIDTH), BF16)],
    )
    back_first = send(top, moved(z=1))
    back_rest = send(after(bottom, back_first, gu2_back), along_loop(1))
    gs = call(add_body, (), (after(gs, top), gs2), [pltpu.VMEM((ROWS, WIDTH), F32)], {0: 0})[0]
    back_turned = send(after(back_first, gu2_back), last_hop(1))
    ga_got = send(after(ga2, top), swap)
    ga = call(add_body, (), (ga, ga_got), [grad_shape(F32)], {0: 0})[0]
    grad_texts = call(text_body, (), (gs, gu1_back, gu2_back), [jax.ShapeDtypeStruct((ROWS, WIDTH), BF16)])[0]
    grad_images, row_loss = call(
        image_body, (flag(0),), (ga, back_first, back_turned, back_rest),
        [jax.ShapeDtypeStruct((ROWS, WIDTH), BF16), jax.ShapeDtypeStruct((1, ROWS), F32)],
    )
    return row_loss[0], grad_images, grad_texts


def solution(mesh):
    in_specs = (P(AXES, None), P(AXES, None), P(AXES), P(), P())
    out_specs = (P(AXES), P(AXES, None), P(AXES, None))
    return jax.shard_map(body, mesh=mesh, in_specs=in_specs, out_specs=out_specs, check_vma=False)
```

```python
import functools
import jax
import jax.numpy as jnp
from jax import lax
from jax.experimental import pallas as pl
from jax.experimental.pallas import tpu as pltpu
from jax.sharding import PartitionSpec as P

AXES = ("dp", "rep")
NT = (((1,), (1,)), ((), ()))
TN = (((0,), (0,)), ((), ()))
F32, BF16 = jnp.float32, jnp.bfloat16


def place(flat):
    dp, rep = divmod(flat, 4)
    return dp // 8, (rep // 2) * 2 + (dp // 4) % 2, dp % 4, rep % 2


def flat_of(y, x, z, core):
    return (y * 8 + (x % 2) * 4 + z) * 4 + (x // 2) * 2 + core


def moved(x=0, z=0, core=0):
    route = []
    for source in range(128):
        sy, sx, sz, sc = place(source)
        route.append((source, flat_of(sy, (sx + x) % 4, (sz + z) % 4, (sc + core) % 2)))
    return route


def along_loop(step, core=0):
    return [(source, ((source + 4 * step) % 128) ^ core) for source in range(128)]


def last_hop(step):
    along_z = dict(moved(z=step))
    turn = 3 if step > 0 else 0
    return [(along_z[s], d) for s, d in along_loop(step) if place(s)[2] == turn]


def send(block, route):
    return lax.ppermute(block, AXES, route)


def after(block, *others):
    return lax.optimization_barrier((block, *others))[0]


def terms(dots, positive, temper, shift):
    logit = temper * dots + shift
    z = jnp.where(positive, -logit, logit)
    e = jnp.exp(-jnp.abs(z))
    log_term = jnp.where(e < 1e-4, (1.0 - 0.5 * e) * e, jnp.log(1.0 + e))
    loss = jnp.maximum(z, 0.0) + log_term
    sigmoid = jnp.exp(jnp.minimum(z, 0.0) - log_term)
    coef = (jnp.where(positive, -temper, temper) * sigmoid).astype(BF16)
    return loss, coef


SMEM = pl.BlockSpec(memory_space=pltpu.SMEM)
VMEM = pl.BlockSpec(memory_space=pltpu.VMEM)
ROWS, WIDTH, HALF = 512, 1152, 256
FIRST = 256
CARRY = 16


def near(array):
    return pltpu.with_memory_space_constraint(array, pltpu.VMEM)


def call(kernel, smalls, arrays, outs, alias=None, cells=0):
    return pl.pallas_call(
        kernel,
        in_specs=[SMEM] * len(smalls) + [VMEM] * len(arrays),
        out_specs=[VMEM] * len(outs),
        out_shape=outs,
        input_output_aliases=alias or {},
        compiler_params=pltpu.CompilerParams(vmem_limit_bytes=16 << 20),
        cost_estimate=pl.CostEstimate(flops=1000, bytes_accessed=1000, transcendentals=0),
    )(*smalls, *map(near, arrays))


def split3(value):
    high = value.astype(BF16)
    middle = (value - high.astype(F32)).astype(BF16)
    low = (value - high.astype(F32) - middle.astype(F32)).astype(BF16)
    return high, middle, low


def put_loss(ref, at, loss):
    if ref.dtype == F32:
        ref[pl.ds(at, 8), :ROWS] = jnp.broadcast_to(loss, (8, ROWS))
        return
    row = lax.broadcasted_iota(jnp.int32, (CARRY, ROWS), 0)
    parts = [part.astype(F32) for part in split3(loss)]
    block = jnp.where(row == 0, parts[0], jnp.where(row == 1, parts[1], jnp.where(row == 2, parts[2], 0.0)))
    ref[pl.ds(at, CARRY), :ROWS] = block.astype(BF16)


def get_loss(ref, at):
    if ref.dtype == F32:
        return ref[pl.ds(at, 8), :ROWS][0:1]
    parts = ref[pl.ds(at, CARRY), :ROWS].astype(F32)
    return parts[0:1] + parts[1:2] + parts[2:3]


def pair_body(n, gi_has, gt_has, start_ref, scale_ref, offset_ref, *refs):
    refs = list(refs)

    def take(count):
        out = refs[:count]
        del refs[:count]
        return out

    imgs, txt = take(n), take(1)[0]
    gi_in = take(n) if gi_has else None
    gt_in = take(1)[0] if gt_has else None
    gi, gt = take(n), take(1)[0]
    temper, shift = scale_ref[0], offset_ref[0]
    t = txt[...]
    col = start_ref[0] + lax.broadcasted_iota(jnp.int32, (t.shape[0], ROWS), 0).astype(F32)
    t_sum = None
    for m in range(n):
        a = imgs[m][:ROWS, :]
        code = imgs[m][pl.ds(ROWS, CARRY), :ROWS].astype(F32)
        partner = code[0:1] * 256.0 + code[1:2]
        dots = lax.dot_general(t, a, NT, preferred_element_type=F32)
        ls, coef = terms(dots, partner == col, temper, shift)
        loss = jnp.sum(ls, axis=0, keepdims=True)
        g = lax.dot_general(coef, t, TN, preferred_element_type=F32)
        d = jnp.dot(coef, a, preferred_element_type=F32)
        if gi_has:
            loss = loss + get_loss(gi_in[m], ROWS)
            g = g + gi_in[m][:ROWS, :]
        gi[m][:ROWS, :] = g.astype(gi[m].dtype)
        put_loss(gi[m], ROWS, loss)
        t_sum = d if t_sum is None else t_sum + d
    if gt_has:
        t_sum = t_sum + gt_in[...]
    gt[...] = t_sum.astype(gt.dtype)


def grad_shape(ty):
    return pltpu.VMEM((ROWS + (8 if ty == F32 else CARRY), WIDTH), ty)


def pairs(imgs, txt, start, scale, offset, gi=None, gi_types=None, gt=None, gt_type=F32):
    n = len(imgs)
    gi_types = gi_types or [F32] * n
    alias = {4 + n + m: m for m in range(n) if gi is not None and gi_types[m] == F32}
    outs = [grad_shape(ty) for ty in gi_types] + [pltpu.VMEM(txt.shape, gt_type)]
    got = call(
        functools.partial(pair_body, n, gi is not None, gt is not None),
        (start, scale, offset),
        [*imgs, txt, *(gi or []), *([gt] if gt is not None else [])],
        outs,
        alias,
    )
    return got[:n], got[n]


def assemble_body(flag_ref, first, turned, rest, out):
    out[:HALF, :] = jnp.where(flag_ref[0] == 1, turned[...], first[...])
    out[HALF:, :] = rest[...]


def fold_body(mine, other, top, rest):
    top[...] = (mine[:HALF, :] + other[:HALF, :].astype(F32)).astype(BF16)
    rest[:HALF, :] = (mine[HALF:ROWS, :] + other[HALF:ROWS, :].astype(F32)).astype(BF16)
    put_loss(rest, HALF, get_loss(mine, ROWS) + get_loss(other, ROWS))


def image_body(flag_ref, mine, first, turned, rest, grad, row_loss):
    top = jnp.where(flag_ref[0] == 1, turned[...], first[...]).astype(F32)
    grad[:HALF, :] = (mine[:HALF, :] + top).astype(BF16)
    grad[HALF:, :] = (mine[HALF:ROWS, :] + rest[:HALF, :].astype(F32)).astype(BF16)
    loss = get_loss(mine, ROWS) + get_loss(rest, HALF)
    row_loss[...] = loss / (8.0 * ROWS)


def add_body(one, two, out):
    out[...] = one[...] + two[...]


def text_body(mine, back1, back2, grad):
    grad[:FIRST, :] = (mine[:FIRST, :] + back1[...].astype(F32)).astype(BF16)
    grad[FIRST:, :] = (mine[FIRST:, :] + back2[...].astype(F32)).astype(BF16)


def body(images, texts, partner, scale, offset):
    dp, rep = lax.axis_index("dp"), lax.axis_index("rep")
    start = ((dp * 4 + rep) * ROWS).astype(F32)[None]
    far_start = ((dp * 4 + (rep ^ 2)) * ROWS).astype(F32)[None]
    swap = moved(core=1)
    across = moved(x=2)

    def flag(z):
        return (dp % 4 == z).astype(jnp.int32)[None]

    code = jnp.stack([partner // 256, partner % 256]).astype(BF16)
    own = jnp.concatenate([images, jnp.pad(code, ((0, CARRY - 2), (0, WIDTH - ROWS)))])
    far1 = send(texts[:FIRST], across)
    first = send(images[:HALF], moved(z=-1))
    own2 = send(own, swap)
    (ga, ga2), gs = pairs([own, own2], texts, start, scale, offset)
    rest = send(after(own[HALF:], first, ga2, far1), along_loop(-1))
    turned = send(after(first, ga2, far1), last_hop(-1))
    (ga, ga2), gu = pairs([own, own2], far1, far_start, scale, offset, [ga, ga2])
    far2 = send(after(texts[FIRST:], far1), across)
    visitor = call(
        assemble_body, (flag(3),), (after(first, gu), turned, rest), [pltpu.VMEM((ROWS + CARRY, WIDTH), BF16)]
    )[0]
    visitor2 = send(visitor, swap)
    (gb, gb2), gs2 = pairs([visitor, visitor2], texts, start, scale, offset)
    (gb, gb2), gu = pairs([visitor, visitor2], far1, far_start, scale, offset, [gb, gb2], None, gu, BF16)
    every = [own, own2, visitor, visitor2]
    gu1_back = send(gu, across)
    (ga, ga2, gb, gb2), gu2 = pairs(
        every, far2, far_start + FIRST, scale, offset, [ga, ga2, gb, gb2], [F32, F32, F32, BF16], None, BF16
    )
    gu2_back = send(gu2, across)
    gb_got = send(after(gb2, gu1_back), swap)
    top, bottom = call(
        fold_body, (), (gb, gb_got),
        [pltpu.VMEM((HALF, WIDTH), BF16), pltpu.VMEM((HALF + CARRY, WIDTH), BF16)],
    )
    back_first = send(top, moved(z=1))
    back_rest = send(after(bottom, back_first, gu2_back), along_loop(1))
    gs = call(add_body, (), (after(gs, top), gs2), [pltpu.VMEM((ROWS, WIDTH), F32)], {0: 0})[0]
    back_turned = send(after(back_first, gu2_back), last_hop(1))
    ga_got = send(after(ga2, top), swap)
    ga = call(add_body, (), (ga, ga_got), [grad_shape(F32)], {0: 0})[0]
    grad_texts = call(text_body, (), (gs, gu1_back, gu2_back), [jax.ShapeDtypeStruct((ROWS, WIDTH), BF16)])[0]
    grad_images, row_loss = call(
        image_body, (flag(0),), (ga, back_first, back_turned, back_rest),
        [jax.ShapeDtypeStruct((ROWS, WIDTH), BF16), jax.ShapeDtypeStruct((1, ROWS), F32)],
    )
    return row_loss[0], grad_images, grad_texts


def solution(mesh):
    in_specs = (P(AXES, None), P(AXES, None), P(AXES), P(), P())
    out_specs = (P(AXES), P(AXES, None), P(AXES, None))
    return jax.shard_map(body, mesh=mesh, in_specs=in_specs, out_specs=out_specs, check_vma=False)
```
